32 devices in a mesh: grp: 2 (over y), energy: 4 (over z), atom: 2 (over x), kz: 2 (over core).
Axes of the slice: x: 2, y: 2, z: 4, core: 2. Of those that a mesh axis runs over, the one named last changes fastest.
Arguments:
- green: float32 [8, 32, 512, 512], P(('grp', 'kz'), 'energy', 'atom'), parts along dimension 0, may hold values from -6 to 6
- couplings: float32 [4, 512, 512], P('atom'), may hold values from -0.25 to 0.25
- occupation: float32 [3], replicated, may hold values from 0.05 to 2
- offsets: int32 [3], replicated, may hold values from 1 to 16, as said below
- owners: int32 [3], replicated, may hold values from 0 to 3
Outputs:
- sigma: float32 [1024, 32, 512], P(('grp', 'atom', 'kz'), 'energy'), parts along dimension 0
The draws below stay inside these ranges and needn't reach their ends.
There are 2 independent parts, one for each index of `grp`. The reference program is written for one: setup_inputs(seed, part) draws one part's arguments, and reference() takes and returns one part's arrays. A program takes and returns all parts, laid end to end along the dimension named above; an argument that names none is the same for every part. Nothing has to cross between parts.
Inputs may be any that keep to these rules, and one draw needn't show every extreme that they name: `offsets`: one mode's offset is exactly 16.
All inputs are finite; a program needn't handle non-finite values.
Results may differ from the reference program's by a relative error of at most 0.0001.
Values sent between devices are 32-bit elements; how exact they have to be, the bound alone decides.
A program may use at most 192 MiB of HBM per device.

```python
import math
import jax
import jax.numpy as jnp
from jax import lax

B = 512
MODES = 3
E_DEV = 8
NE = 32
KPTS = 4
NCOUP = 4


def draw_offsets(key, part):
    rest_key = jax.random.fold_in(key, 12)
    order_key = jax.random.fold_in(key, 13)
    leading = jnp.full((1,), 2 * E_DEV, dtype=jnp.int32)
    others = jax.random.randint(rest_key, (MODES - 1,), 1, 2 * E_DEV + 1).astype(jnp.int32)
    values = jnp.concatenate([leading, others]).astype(jnp.int32)
    return jax.random.permutation(order_key, values).astype(jnp.int32)


def shard_levels(stream_key, extent, shards, low, largest):
    loudness, own = 1.0, jax.random.fold_in(stream_key, 6)
    for axis_at, blocks in shards:
        heights = jnp.exp(jax.random.uniform(jax.random.fold_in(own, axis_at), (blocks,), jnp.float32, low / len(shards), largest / len(shards)))
        loudness = loudness * jnp.repeat(heights, extent[axis_at] // blocks).reshape([-1 if axis == axis_at else 1 for axis in range(len(extent))])
    return loudness


def scatter_about(own_key, dims, width, limit, shards=(), kind=jnp.bfloat16):
    drawn = jax.random.normal(own_key, dims, jnp.float32) * width
    if len(shards) > 0:
        drawn = shard_levels(own_key, dims, shards, -0.22, 0.18) * drawn
    return jnp.clip(drawn, min=-limit, max=limit).astype(kind)


def setup_inputs(seed: int = 0, part: int = 0) -> dict:
    arg_keys = jax.random.split(jax.random.key(seed), 6)
    part_splits = jax.random.split(jax.random.fold_in(arg_keys[5], part), 6)
    return {
        "green": scatter_about(part_splits[0], (KPTS, NE, B, B), 1.0, 6.0, ((0, 2), (1, 4), (2, 2)), jnp.float32),
        "couplings": scatter_about(arg_keys[1], (NCOUP, B, B), B ** -0.5, 0.25, ((0, 2),), jnp.float32),
        "occupation": jnp.clip(jnp.exp(jax.random.uniform(arg_keys[2], (MODES,), jnp.float32, math.log(0.05), math.log(2.0))), 0.05, 2.0),
        "offsets": draw_offsets(jax.random.fold_in(arg_keys[5], 71), part),
        "owners": jax.random.randint(arg_keys[4], (MODES,), 0, NCOUP).astype(jnp.int32),
    }


def reference(green, couplings, occupation, offsets, owners):
    summed = jnp.sum(green, axis=0)
    total = jnp.zeros((B, NE, B), jnp.float32)
    for mode in range(MODES):
        coupling = couplings[owners[mode]]
        upper = jnp.roll(summed, -offsets[mode], axis=0)
        lower = jnp.roll(summed, offsets[mode], axis=0)
        weight = occupation[mode]
        combined = ((1.0 + weight) * upper + weight * lower) / KPTS
        product = jnp.einsum("ebc,dc->ebd", combined, coupling, precision=lax.Precision.HIGHEST)
        total = total + jnp.einsum("ab,ebd->aed", coupling, product, precision=lax.Precision.HIGHEST)
    return total
```

```python
import functools
import math

import jax
import jax.numpy as jnp
from jax import lax
from jax.experimental import pallas as pl
from jax.experimental.pallas import tpu as pltpu
from jax.sharding import PartitionSpec as P

MODES = 3
REACH = 2
MESH = pl.DeviceIdType.MESH
F32, BF16 = jnp.float32, jnp.bfloat16


def split(x):
    high = x.astype(BF16)
    return high, (x - high.astype(F32)).astype(BF16)


def dot(x, y):
    return jnp.dot(x, y, preferred_element_type=F32)


def dot3(x, y):
    return dot(x[0], y[0]) + (dot(x[0], y[1]) + dot(x[1], y[0]))


def kernel(
    sizes, green, coup, occ, offs, owners, res,
    grid, raw, mine, theirs, table, cth, ctl, cah, cal, part,
    raw_sem, tab_sem, tab_send, tab_recv, k_send, k_recv,
    z_send, z_recv, s_send, s_recv, o_sem, o_send, o_recv,
):
    ne, na, nk, chunks = sizes
    mom, edev, brows, order = green.shape
    rows_table = coup.shape[0]
    momenta = mom * nk
    line = ne <= 2 * REACH
    slots = ne if line else 2 * REACH + 1
    hops = ne - 1 if line else REACH
    half = brows // nk
    ce = edev // chunks
    emine = edev // nk
    rows_out = order // (na * nk)
    p, a, k = (lax.axis_index(n) for n in ("energy", "atom", "kz"))
    right, left = lax.rem(p + 1, ne), lax.rem(p + ne - 1, ne)

    def when(condition, action):
        if line:
            pl.when(condition)(action)
        else:
            action()

    def raw_copy(c):
        es = pl.ds(c * ce, ce)
        return pltpu.make_async_copy(green.at[:, es], raw.at[:, es], raw_sem.at[c])

    for c in range(chunks):
        raw_copy(c).start()
    tab_local = pltpu.make_async_copy(coup, table.at[pl.ds(a * rows_table, rows_table)], tab_sem)
    tab_local.start()

    barrier = pltpu.get_barrier_semaphore()

    def greet(where):
        pl.semaphore_signal(barrier, inc=1, device_id=where, device_id_type=MESH)

    when(p + 1 < ne, lambda: greet({"energy": right}))
    when(p >= 1, lambda: greet({"energy": left}))
    me = a * nk + k
    peers = na * nk

    def peer(j):
        q = lax.rem(me + j, peers)
        return q, {"atom": q // nk, "kz": lax.rem(q, nk)}

    for j in range(1, peers):
        greet(peer(j)[1])
    if line:
        beside = jnp.where(p + 1 < ne, 1, 0) + jnp.where(p >= 1, 1, 0)
    else:
        beside = 2
    pl.semaphore_wait(barrier, peers - 1 + beside)

    def remote(src, dst, send, recv, where):
        return pltpu.make_async_remote_copy(
            src_ref=src, dst_ref=dst, send_sem=send, recv_sem=recv,
            device_id=where, device_id_type=MESH,
        )

    def tab_copy(j):
        return remote(
            coup, table.at[pl.ds(a * rows_table, rows_table)], tab_send.at[j - 1], tab_recv.at[j - 1],
            {"atom": lax.rem(a + j, na)},
        )

    def tab_arrival(j):
        source = lax.rem(a + na - j, na)
        return remote(
            coup, table.at[pl.ds(source * rows_table, rows_table)], tab_send.at[j - 1], tab_recv.at[j - 1],
            {"atom": lax.rem(a + j, na)},
        )

    def k_copy(j, c):
        es = pl.ds(c * ce, ce)
        return remote(
            mine.at[es], theirs.at[j - 1, es], k_send.at[j - 1, c], k_recv.at[j - 1, c],
            {"kz": lax.rem(k + j, nk)},
        )

    my_rows = pl.ds(pl.multiple_of(k * half, half), half)

    def z_copy(d, h, c):
        s, t = ((slots - h + 1) % slots, (slots - h) % slots) if d == 0 else (h - 1, h)
        return remote(
            grid.at[pl.ds(s * edev + c * ce, ce), my_rows], grid.at[pl.ds(t * edev + c * ce, ce), my_rows],
            z_send.at[d, h - 1, c], z_recv.at[d, h - 1, c], {"energy": right if d == 0 else left},
        )

    def sends(d, h):
        if d == 0:
            return jnp.logical_and(p - h + 1 >= 0, p + 1 < ne)
        return jnp.logical_and(p + h - 1 < ne, p >= 1)

    def receives(d, h):
        return p - h >= 0 if d == 0 else p + h < ne

    def share_copy(j, d, h, c, rows):
        t = (slots - h) % slots if d == 0 else h
        at = grid.at[pl.ds(t * edev + c * ce, ce), rows]
        return remote(
            at, at, s_send.at[j - 1, d, h - 1, c], s_recv.at[j - 1, d, h - 1, c],
            {"kz": lax.rem(k + j, nk)},
        )

    def share_arrival(j, d, h, c):
        source = lax.rem(k + nk - j, nk)
        return share_copy(j, d, h, c, pl.ds(pl.multiple_of(source * half, half), half))

    for j in range(1, na):
        tab_copy(j).start()
    for c in range(chunks):
        raw_copy(c).wait()
        for e in range(c * ce, (c + 1) * ce):
            total = raw[0, e]
            for i in range(1, mom):
                total = total + raw[i, e]
            mine[e] = total
        for j in range(1, nk):
            k_copy(j, c).start()
    for c in range(chunks):
        for j in range(1, nk):
            k_copy(j, c).wait_recv()
        for e in range(c * ce, (c + 1) * ce):
            total = mine[e]
            for j in range(1, nk):
                total = total + theirs[j - 1, e]
            grid[e] = total
        for d in range(2):
            when(sends(d, 1), lambda d=d, c=c: z_copy(d, 1, c).start())

    tab_local.wait()
    for j in range(1, na):
        tab_arrival(j).wait_recv()
    for m in range(MODES):
        owner = owners[m]
        high, low = split(table[owner].T)
        cth[m] = high
        ctl[m] = low
        high, low = split(table[owner, :, pl.ds(pl.multiple_of(a * brows, brows), brows)])
        cah[m] = high
        cal[m] = low

    for h in range(1, hops + 1):
        for c in range(chunks):
            for d in range(2):

                def arrived(d=d, h=h, c=c):
                    z_copy(d, h, c).wait_recv()
                    for j in range(1, nk):
                        share_copy(j, d, h, c, my_rows).start()

                when(receives(d, h), arrived)
                if h < hops:
                    when(sends(d, h + 1), lambda d=d, h=h, c=c: z_copy(d, h + 1, c).start())
    for h in range(1, hops + 1):
        for c in range(chunks):
            for d in range(2):
                for j in range(1, nk):
                    when(receives(d, h), lambda j=j, d=d, h=h, c=c: share_arrival(j, d, h, c).wait_recv())

    span = slots * edev

    def o_copy(j, i):
        q, where = peer(j)
        return remote(
            part.at[i, pl.ds(pl.multiple_of(q * rows_out, rows_out), rows_out)], res.at[me, i],
            o_send.at[j - 1, i], o_recv.at[j - 1, i], where,
        )

    def o_arrival(j, i):
        source = lax.rem(me + peers - j, peers)
        return remote(
            part.at[i, pl.ds(0, rows_out)], res.at[source, i],
            o_send.at[j - 1, i], o_recv.at[j - 1, i], peer(j)[1],
        )

    def o_local(i):
        return pltpu.make_async_copy(
            part.at[i, pl.ds(pl.multiple_of(me * rows_out, rows_out), rows_out)], res.at[me, i], o_sem.at[i]
        )

    for i in range(emine):
        e = k * emine + i
        for m in range(MODES):
            weight, step = occ[m], offs[m]
            upper = grid[lax.rem(e + step, span)]
            lower = grid[lax.rem(e - step + span, span)]
            combined = ((1.0 + weight) * upper + weight * lower) / momenta
            product = dot3(split(combined), (cth[m], ctl[m]))
            term = dot3((cah[m], cal[m]), split(product))
            if m == 0:
                part[i] = term
            else:
                part[i] += term
        for j in range(1, peers):
            o_copy(j, i).start()
        o_local(i).start()

    for j in range(1, na):
        tab_copy(j).wait_send()
    for c in range(chunks):
        for j in range(1, nk):
            k_copy(j, c).wait_send()
        for h in range(1, hops + 1):
            for d in range(2):
                when(sends(d, h), lambda d=d, h=h, c=c: z_copy(d, h, c).wait_send())
                for j in range(1, nk):
                    when(receives(d, h), lambda j=j, d=d, h=h, c=c: share_copy(j, d, h, c, my_rows).wait_send())
    for i in range(emine):
        o_local(i).wait()
        for j in range(1, peers):
            o_copy(j, i).wait_send()
            o_arrival(j, i).wait_recv()


def shards(green, couplings, occupation, offsets, owners):
    mom, edev, brows, order = green.shape
    ne, na, nk = (lax.axis_size(n) for n in ("energy", "atom", "kz"))
    chunks = math.gcd(edev, 4)
    line = ne <= 2 * REACH
    slots = ne if line else 2 * REACH + 1
    hops = ne - 1 if line else REACH
    emine, rows_out = edev // nk, order // (na * nk)
    dma = pltpu.SemaphoreType.DMA
    smem = pl.BlockSpec(memory_space=pltpu.SMEM)
    hbm = pl.BlockSpec(memory_space=pl.ANY)
    parts = pl.pallas_call(
        functools.partial(kernel, (ne, na, nk, chunks)),
        out_shape=jax.ShapeDtypeStruct((na * nk, emine, rows_out, order), F32),
        in_specs=[hbm, hbm, smem, smem, smem],
        out_specs=hbm,
        scratch_shapes=[
            pltpu.VMEM((slots * edev, brows, order), F32),
            pltpu.VMEM((mom, edev, brows, order), F32),
            pltpu.VMEM((edev, brows, order), F32),
            pltpu.VMEM((nk - 1, edev, brows, order), F32),
            pltpu.VMEM((couplings.shape[0] * na, order, order), F32),
            pltpu.VMEM((MODES, order, order), BF16),
            pltpu.VMEM((MODES, order, order), BF16),
            pltpu.VMEM((MODES, order, brows), BF16),
            pltpu.VMEM((MODES, order, brows), BF16),
            pltpu.VMEM((emine, order, order), F32),
            dma((chunks,)),
            dma,
            dma((na - 1,)),
            dma((na - 1,)),
            dma((nk - 1, chunks)),
            dma((nk - 1, chunks)),
            dma((2, hops, chunks)),
            dma((2, hops, chunks)),
            dma((nk - 1, 2, hops, chunks)),
            dma((nk - 1, 2, hops, chunks)),
            dma((emine,)),
            dma((na * nk - 1, emine)),
            dma((na * nk - 1, emine)),
        ],
        compiler_params=pltpu.CompilerParams(
            collective_id=0, has_side_effects=True, vmem_limit_bytes=58 << 20
        ),
        cost_estimate=pl.CostEstimate(
            flops=12 * MODES * emine * 2 * brows * order * order,
            bytes_accessed=4 * (mom * edev * brows * order + couplings.size + na * nk * emine * rows_out * order),
            transcendentals=0,
        ),
    )(green, couplings, occupation, offsets, owners)
    sigma = jnp.sum(parts.reshape(na, edev, rows_out, order), axis=0)
    return jnp.swapaxes(sigma, 0, 1)


def solution(mesh):
    return jax.shard_map(
        shards,
        mesh=mesh,
        in_specs=(P(("grp", "kz"), "energy", "atom", None), P("atom", None, None), P(), P(), P()),
        out_specs=P(("grp", "atom", "kz"), "energy", None),
        check_vma=False,
    )
```

```python
import functools
import math

import jax
import jax.numpy as jnp
from jax import lax
from jax.experimental import pallas as pl
from jax.experimental.pallas import tpu as pltpu
from jax.sharding import PartitionSpec as P

MODES = 3
REACH = 2
MESH = pl.DeviceIdType.MESH
F32, BF16 = jnp.float32, jnp.bfloat16


def split(x):
    high = x.astype(BF16)
    return high, (x - high.astype(F32)).astype(BF16)


def dot(x, y):
    return jnp.dot(x, y, preferred_element_type=F32)


def dot3(x, y):
    return dot(x[0], y[0]) + (dot(x[0], y[1]) + dot(x[1], y[0]))


def kernel(
    sizes, green, coup, occ, offs, owners, res,
    grid, raw, mine, theirs, table, cth, ctl, cah, cal, part, other, crh, crl, fpart,
    raw_sem, tab_sem, tab_send, tab_recv, k_send, k_recv,
    z_send, z_recv, s_send, s_recv, o_sem, o_send, o_recv,
    x_send, x_recv, xs_send, xs_recv, f_send, f_recv,
):
    ne, na, nk, chunks = sizes
    mom, edev, brows, order = green.shape
    rows_table = coup.shape[0]
    momenta = mom * nk
    line = ne <= 2 * REACH
    slots = ne if line else 2 * REACH + 1
    hops = min(ne - 1, REACH)
    far = line and ne - 1 > REACH
    half = brows // nk
    ce = edev // chunks
    emine = edev // nk
    rows_out = order // (na * nk)
    p, a, k = (lax.axis_index(n) for n in ("energy", "atom", "kz"))
    right, left = lax.rem(p + 1, ne), lax.rem(p + ne - 1, ne)
    beside_end = jnp.logical_and(p >= 1, p + 1 < ne)
    at_end = jnp.logical_or(p < 1, p + 1 >= ne)
    partner = lax.rem((ne - 1) * (p - 1) + ne * ne, ne)

    def when(condition, action):
        if line:
            pl.when(condition)(action)
        else:
            action()

    def raw_copy(c):
        es = pl.ds(c * ce, ce)
        return pltpu.make_async_copy(green.at[:, es], raw.at[:, es], raw_sem.at[c])

    for c in range(chunks):
        raw_copy(c).start()
    tab_local = pltpu.make_async_copy(coup, table.at[pl.ds(a * rows_table, rows_table)], tab_sem)
    tab_local.start()

    barrier = pltpu.get_barrier_semaphore()

    def greet(where):
        pl.semaphore_signal(barrier, inc=1, device_id=where, device_id_type=MESH)

    when(p + 1 < ne, lambda: greet({"energy": right}))
    when(p >= 1, lambda: greet({"energy": left}))
    me = a * nk + k
    peers = na * nk

    def peer(j):
        q = lax.rem(me + j, peers)
        return q, {"atom": q // nk, "kz": lax.rem(q, nk)}

    for j in range(1, peers):
        greet(peer(j)[1])
    if line:
        beside = jnp.where(p + 1 < ne, 1, 0) + jnp.where(p >= 1, 1, 0)
    else:
        beside = 2
    if far:
        for j in range(1, nk):
            greet({"energy": partner, "kz": lax.rem(k + j, nk)})
        beside = beside + nk - 1
    pl.semaphore_wait(barrier, peers - 1 + beside)

    def remote(src, dst, send, recv, where):
        return pltpu.make_async_remote_copy(
            src_ref=src, dst_ref=dst, send_sem=send, recv_sem=recv,
            device_id=where, device_id_type=MESH,
        )

    def tab_copy(j):
        return remote(
            coup, table.at[pl.ds(a * rows_table, rows_table)], tab_send.at[j - 1], tab_recv.at[j - 1],
            {"atom": lax.rem(a + j, na)},
        )

    def tab_arrival(j):
        source = lax.rem(a + na - j, na)
        return remote(
            coup, table.at[pl.ds(source * rows_table, rows_table)], tab_send.at[j - 1], tab_recv.at[j - 1],
            {"atom": lax.rem(a + j, na)},
        )

    def k_copy(j, c):
        es = pl.ds(c * ce, ce)
        return remote(
            mine.at[es], theirs.at[j - 1, es], k_send.at[j - 1, c], k_recv.at[j - 1, c],
            {"kz": lax.rem(k + j, nk)},
        )

    my_rows = pl.ds(pl.multiple_of(k * half, half), half)

    def z_copy(d, h, c):
        s, t = ((slots - h + 1) % slots, (slots - h) % slots) if d == 0 else (h - 1, h)
        return remote(
            grid.at[pl.ds(s * edev + c * ce, ce), my_rows], grid.at[pl.ds(t * edev + c * ce, ce), my_rows],
            z_send.at[d, h - 1, c], z_recv.at[d, h - 1, c], {"energy": right if d == 0 else left},
        )

    def sends(d, h):
        if d == 0:
            return jnp.logical_and(p - h + 1 >= 0, p + 1 < ne)
        return jnp.logical_and(p + h - 1 < ne, p >= 1)

    def receives(d, h):
        return p - h >= 0 if d == 0 else p + h < ne

    def share_copy(j, d, h, c, rows):
        t = (slots - h) % slots if d == 0 else h
        at = grid.at[pl.ds(t * edev + c * ce, ce), rows]
        return remote(
            at, at, s_send.at[j - 1, d, h - 1, c], s_recv.at[j - 1, d, h - 1, c],
            {"kz": lax.rem(k + j, nk)},
        )

    def share_arrival(j, d, h, c):
        source = lax.rem(k + nk - j, nk)
        return share_copy(j, d, h, c, pl.ds(pl.multiple_of(source * half, half), half))

    def x_copy(j, c):
        return remote(
            grid.at[pl.ds(REACH * edev + c * ce, ce), my_rows], other.at[j - 1, pl.ds(c * ce, ce), my_rows],
            x_send.at[j - 1, c], x_recv.at[j - 1, c], {"atom": lax.rem(a + j, na)},
        )

    def xs_copy(j, i, c, rows):
        at = other.at[j - 1, pl.ds(c * ce, ce), rows]
        return remote(
            at, at, xs_send.at[j - 1, i - 1, c], xs_recv.at[j - 1, i - 1, c], {"kz": lax.rem(k + i, nk)}
        )

    def xs_arrival(j, i, c):
        source = lax.rem(k + nk - i, nk)
        return xs_copy(j, i, c, pl.ds(pl.multiple_of(source * half, half), half))

    def far_here(d):
        if d == 0:
            return jnp.logical_and(p >= REACH, p + 1 < ne)
        return jnp.logical_and(p + REACH < ne, p >= 1)

    for j in range(1, na):
        tab_copy(j).start()
    for c in range(chunks):
        raw_copy(c).wait()
        for e in range(c * ce, (c + 1) * ce):
            total = raw[0, e]
            for i in range(1, mom):
                total = total + raw[i, e]
            mine[e] = total
        for j in range(1, nk):
            k_copy(j, c).start()
    for c in range(chunks):
        for j in range(1, nk):
            k_copy(j, c).wait_recv()
        for e in range(c * ce, (c + 1) * ce):
            total = mine[e]
            for j in range(1, nk):
                total = total + theirs[j - 1, e]
            grid[e] = total
        for d in range(2):
            when(sends(d, 1), lambda d=d, c=c: z_copy(d, 1, c).start())

    tab_local.wait()
    for j in range(1, na):
        tab_arrival(j).wait_recv()
    for m in range(MODES):
        owner = owners[m]
        high, low = split(table[owner].T)
        cth[m] = high
        ctl[m] = low
        high, low = split(table[owner, :, pl.ds(pl.multiple_of(a * brows, brows), brows)])
        cah[m] = high
        cal[m] = low
        if far:
            for j in range(na):
                columns = pl.ds(pl.multiple_of(lax.rem(a + na - j, na) * brows, brows), brows)
                rows = pl.ds(pl.multiple_of(a * brows, brows), brows)
                high, low = split(table[owner, rows, columns])
                crh[m * na + j] = high
                crl[m * na + j] = low

    for h in range(1, hops + 1):
        for c in range(chunks):
            for d in range(2):

                def arrived(d=d, h=h, c=c):
                    z_copy(d, h, c).wait_recv()
                    for j in range(1, nk):
                        share_copy(j, d, h, c, my_rows).start()

                when(receives(d, h), arrived)
                if far and h == hops:

                    def spread(c=c):
                        for j in range(1, na):
                            x_copy(j, c).start()

                    pl.when(far_here(d))(spread)
                if h < hops:
                    when(sends(d, h + 1), lambda d=d, h=h, c=c: z_copy(d, h + 1, c).start())
    if far:

        @pl.when(beside_end)
        def _():
            for c in range(chunks):
                for j in range(1, na):
                    x_copy(j, c).wait_recv()
                    for i in range(1, nk):
                        xs_copy(j, i, c, my_rows).start()

    for h in range(1, hops + 1):
        for c in range(chunks):
            for d in range(2):
                for j in range(1, nk):
                    when(receives(d, h), lambda j=j, d=d, h=h, c=c: share_arrival(j, d, h, c).wait_recv())

    span = slots * edev

    def o_copy(j, i):
        q, where = peer(j)
        return remote(
            part.at[i, pl.ds(pl.multiple_of(q * rows_out, rows_out), rows_out)], res.at[me, i],
            o_send.at[j - 1, i], o_recv.at[j - 1, i], where,
        )

    def o_arrival(j, i):
        source = lax.rem(me + peers - j, peers)
        return remote(
            part.at[i, pl.ds(0, rows_out)], res.at[source, i],
            o_send.at[j - 1, i], o_recv.at[j - 1, i], peer(j)[1],
        )

    def o_local(i):
        return pltpu.make_async_copy(
            part.at[i, pl.ds(pl.multiple_of(me * rows_out, rows_out), rows_out)], res.at[me, i], o_sem.at[i]
        )

    def f_copy(j, i):
        q = lax.rem(k + j, nk)
        return remote(
            fpart.at[i, pl.ds(pl.multiple_of(q * rows_out, rows_out), rows_out)], res.at[peers + k, i],
            f_send.at[j, i], f_recv.at[j, i], {"energy": partner, "kz": q},
        )

    def f_arrival(j, i):
        return remote(
            fpart.at[i, pl.ds(0, rows_out)], res.at[peers + lax.rem(k + nk - j, nk), i],
            f_send.at[j, i], f_recv.at[j, i], {"energy": partner, "kz": lax.rem(k + j, nk)},
        )

    if far:
        missing = jnp.where(p < 1, slots - 1, jnp.where(p + 1 >= ne, 1, -1))

    def seen(index, e, weight):
        if not far:
            return index, weight
        absent = lax.div(index, edev) == missing
        return jnp.where(absent, e, index), jnp.where(absent, 0.0, weight)

    def near(i):
        e = k * emine + i
        for m in range(MODES):
            weight, step = occ[m], offs[m]
            iu, wu = seen(lax.rem(e + step, span), e, 1.0 + weight)
            il, wl = seen(lax.rem(e - step + span, span), e, weight)
            combined = (wu * grid[iu] + wl * grid[il]) / momenta
            product = dot3(split(combined), (cth[m], ctl[m]))
            term = dot3((cah[m], cal[m]), split(product))
            if m == 0:
                part[i] = term
            else:
                part[i] += term
        for j in range(1, peers):
            o_copy(j, i).start()
        o_local(i).start()

    def among(index, weight):
        inside = index < edev
        return jnp.where(inside, index, 0), jnp.where(inside, weight, 0.0)

    def farthest(i):
        e = (ne - 1) * (2 * p - ne + 1) * edev + span + k * emine + i
        for m in range(MODES):
            weight, step = occ[m], offs[m]
            iu, wu = among(lax.rem(e + step, span), 1.0 + weight)
            il, wl = among(lax.rem(e - step + span, span), weight)
            rows = None
            for j in range(na):
                if j == 0:
                    upper, lower = grid[REACH * edev + iu], grid[REACH * edev + il]
                else:
                    upper, lower = other[j - 1, iu], other[j - 1, il]
                combined = (wu * upper + wl * lower) / momenta
                term = dot3((crh[m * na + j], crl[m * na + j]), split(combined))
                rows = term if rows is None else rows + term
            term = dot3(split(rows), (cth[m], ctl[m]))
            if m == 0:
                fpart[i] = term
            else:
                fpart[i] += term
        for j in range(nk):
            f_copy(j, i).start()

    for i in range(emine):
        near(i)
        if far:

            @pl.when(beside_end)
            def _():
                if i == 0:
                    for c in range(chunks):
                        for j in range(1, na):
                            for t in range(1, nk):
                                xs_arrival(j, t, c).wait_recv()
                farthest(i)

    for j in range(1, na):
        tab_copy(j).wait_send()
    for c in range(chunks):
        for j in range(1, nk):
            k_copy(j, c).wait_send()
        for h in range(1, hops + 1):
            for d in range(2):
                when(sends(d, h), lambda d=d, h=h, c=c: z_copy(d, h, c).wait_send())
                for j in range(1, nk):
                    when(receives(d, h), lambda j=j, d=d, h=h, c=c: share_copy(j, d, h, c, my_rows).wait_send())
    if far:

        @pl.when(beside_end)
        def _():
            for c in range(chunks):
                for j in range(1, na):
                    x_copy(j, c).wait_send()
                    for i in range(1, nk):
                        xs_copy(j, i, c, my_rows).wait_send()
            for i in range(emine):
                for j in range(nk):
                    f_copy(j, i).wait_send()

        @pl.when(at_end)
        def _():
            for i in range(emine):
                for j in range(nk):
                    f_arrival(j, i).wait_recv()

    for i in range(emine):
        o_local(i).wait()
        for j in range(1, peers):
            o_copy(j, i).wait_send()
            o_arrival(j, i).wait_recv()


def shards(green, couplings, occupation, offsets, owners):
    mom, edev, brows, order = green.shape
    ne, na, nk = (lax.axis_size(n) for n in ("energy", "atom", "kz"))
    chunks = math.gcd(edev, 4)
    line = ne <= 2 * REACH
    slots = ne if line else 2 * REACH + 1
    hops = min(ne - 1, REACH)
    emine, rows_out = edev // nk, order // (na * nk)
    far = line and ne - 1 > REACH
    extra = nk if far else 0
    f_edev, f_emine, f_brows = (edev, emine, brows) if far else (8, 8, 128)
    f_modes = MODES if far else 1
    dma = pltpu.SemaphoreType.DMA
    smem = pl.BlockSpec(memory_space=pltpu.SMEM)
    hbm = pl.BlockSpec(memory_space=pl.ANY)
    parts = pl.pallas_call(
        functools.partial(kernel, (ne, na, nk, chunks)),
        out_shape=jax.ShapeDtypeStruct((na * nk + extra, emine, rows_out, order), F32),
        in_specs=[hbm, hbm, smem, smem, smem],
        out_specs=hbm,
        scratch_shapes=[
            pltpu.VMEM((slots * edev, brows, order), F32),
            pltpu.VMEM((mom, edev, brows, order), F32),
            pltpu.VMEM((edev, brows, order), F32),
            pltpu.VMEM((nk - 1, edev, brows, order), F32),
            pltpu.VMEM((couplings.shape[0] * na, order, order), F32),
            pltpu.VMEM((MODES, order, order), BF16),
            pltpu.VMEM((MODES, order, order), BF16),
            pltpu.VMEM((MODES, order, brows), BF16),
            pltpu.VMEM((MODES, order, brows), BF16),
            pltpu.VMEM((emine, order, order), F32),
            pltpu.VMEM((na - 1, f_edev, f_brows, order if far else 128), F32),
            pltpu.VMEM((f_modes * na, f_brows, f_brows), BF16),
            pltpu.VMEM((f_modes * na, f_brows, f_brows), BF16),
            pltpu.VMEM((f_emine, f_brows, order if far else 128), F32),
            dma((chunks,)),
            dma,
            dma((na - 1,)),
            dma((na - 1,)),
            dma((nk - 1, chunks)),
            dma((nk - 1, chunks)),
            dma((2, hops, chunks)),
            dma((2, hops, chunks)),
            dma((nk - 1, 2, hops, chunks)),
            dma((nk - 1, 2, hops, chunks)),
            dma((emine,)),
            dma((na * nk - 1, emine)),
            dma((na * nk - 1, emine)),
            dma((na - 1, chunks)),
            dma((na - 1, chunks)),
            dma((na - 1, nk - 1, chunks)),
            dma((na - 1, nk - 1, chunks)),
            dma((nk, emine)),
            dma((nk, emine)),
        ],
        compiler_params=pltpu.CompilerParams(
            collective_id=0, has_side_effects=True, vmem_limit_bytes=58 << 20
        ),
        cost_estimate=pl.CostEstimate(
            flops=12 * MODES * emine * 2 * brows * order * order,
            bytes_accessed=4 * (mom * edev * brows * order + couplings.size + na * nk * emine * rows_out * order),
            transcendentals=0,
        ),
    )(green, couplings, occupation, offsets, owners)
    sigma = jnp.sum(parts[: na * nk].reshape(na, edev, rows_out, order), axis=0)
    if far:
        place = lax.axis_index("energy")
        end = jnp.logical_or(place == 0, place == ne - 1)
        sigma = sigma + jnp.where(end, parts[na * nk :].reshape(edev, rows_out, order), 0.0)
    return jnp.swapaxes(sigma, 0, 1)


def solution(mesh):
    return jax.shard_map(
        shards,
        mesh=mesh,
        in_specs=(P(("grp", "kz"), "energy", "atom", None), P("atom", None, None), P(), P(), P()),
        out_specs=P(("grp", "atom", "kz"), "energy", None),
        check_vma=False,
    )
```

```python
import functools
import math

import jax
import jax.numpy as jnp
from jax import lax
from jax.experimental import pallas as pl
from jax.experimental.pallas import tpu as pltpu
from jax.sharding import PartitionSpec as P

MODES = 3
REACH = 2
MESH = pl.DeviceIdType.MESH
F32, BF16 = jnp.float32, jnp.bfloat16


def split(x):
    high = x.astype(BF16)
    return high, (x - high.astype(F32)).astype(BF16)


def dot(x, y):
    return jnp.dot(x, y, preferred_element_type=F32)


def dot3(x, y):
    return dot(x[0], y[0]) + (dot(x[0], y[1]) + dot(x[1], y[0]))


def kernel(
    sizes, green, coup, occ, offs, owners, res, ends,
    grid, raw, mine, theirs, table, cth, ctl, cah, cal, part, other, crh, crl, fpart,
    raw_sem, tab_sem, tab_send, tab_recv, k_send, k_recv,
    z_send, z_recv, s_send, s_recv, o_sem, o_send, o_recv,
    x_send, x_recv, xs_send, xs_recv, f_send, f_recv,
):
    ne, na, nk, chunks = sizes
    mom, edev, brows, order = green.shape
    rows_table = coup.shape[0]
    momenta = mom * nk
    line = ne <= 2 * REACH
    slots = ne if line else 2 * REACH + 1
    hops = min(ne - 1, REACH)
    far = line and ne - 1 > REACH
    half = brows // nk
    ce = edev // chunks
    emine = edev // nk
    rows_out = order // (na * nk)
    p, a, k = (lax.axis_index(n) for n in ("energy", "atom", "kz"))
    right, left = lax.rem(p + 1, ne), lax.rem(p + ne - 1, ne)
    beside_end = jnp.logical_and(p >= 1, p + 1 < ne)
    at_end = jnp.logical_or(p < 1, p + 1 >= ne)
    partner = lax.rem((ne - 1) * (p - 1) + ne * ne, ne)

    def when(condition, action):
        if line:
            pl.when(condition)(action)
        else:
            action()

    def raw_copy(c):
        es = pl.ds(c * ce, ce)
        return pltpu.make_async_copy(green.at[:, es], raw.at[:, es], raw_sem.at[c])

    for c in range(chunks):
        raw_copy(c).start()
    tab_local = pltpu.make_async_copy(coup, table.at[pl.ds(a * rows_table, rows_table)], tab_sem)
    tab_local.start()

    barrier = pltpu.get_barrier_semaphore()

    def greet(where):
        pl.semaphore_signal(barrier, inc=1, device_id=where, device_id_type=MESH)

    when(p + 1 < ne, lambda: greet({"energy": right}))
    when(p >= 1, lambda: greet({"energy": left}))
    me = a * nk + k
    peers = na * nk

    def peer(j):
        q = lax.rem(me + j, peers)
        return q, {"atom": q // nk, "kz": lax.rem(q, nk)}

    for j in range(1, peers):
        greet(peer(j)[1])
    if line:
        beside = jnp.where(p + 1 < ne, 1, 0) + jnp.where(p >= 1, 1, 0)
    else:
        beside = 2
    if far:
        for j in range(1, nk):
            greet({"energy": partner, "kz": lax.rem(k + j, nk)})
        beside = beside + nk - 1
    pl.semaphore_wait(barrier, peers - 1 + beside)

    def remote(src, dst, send, recv, where):
        return pltpu.make_async_remote_copy(
            src_ref=src, dst_ref=dst, send_sem=send, recv_sem=recv,
            device_id=where, device_id_type=MESH,
        )

    def tab_copy(j):
        return remote(
            coup, table.at[pl.ds(a * rows_table, rows_table)], tab_send.at[j - 1], tab_recv.at[j - 1],
            {"atom": lax.rem(a + j, na)},
        )

    def tab_arrival(j):
        source = lax.rem(a + na - j, na)
        return remote(
            coup, table.at[pl.ds(source * rows_table, rows_table)], tab_send.at[j - 1], tab_recv.at[j - 1],
            {"atom": lax.rem(a + j, na)},
        )

    def k_copy(j, c):
        es = pl.ds(c * ce, ce)
        return remote(
            mine.at[es], theirs.at[j - 1, es], k_send.at[j - 1, c], k_recv.at[j - 1, c],
            {"kz": lax.rem(k + j, nk)},
        )

    my_rows = pl.ds(pl.multiple_of(k * half, half), half)

    def z_copy(d, h, c):
        s, t = ((slots - h + 1) % slots, (slots - h) % slots) if d == 0 else (h - 1, h)
        return remote(
            grid.at[pl.ds(s * edev + c * ce, ce), my_rows], grid.at[pl.ds(t * edev + c * ce, ce), my_rows],
            z_send.at[d, h - 1, c], z_recv.at[d, h - 1, c], {"energy": right if d == 0 else left},
        )

    def sends(d, h):
        if d == 0:
            return jnp.logical_and(p - h + 1 >= 0, p + 1 < ne)
        return jnp.logical_and(p + h - 1 < ne, p >= 1)

    def receives(d, h):
        return p - h >= 0 if d == 0 else p + h < ne

    def share_copy(j, d, h, c, rows):
        t = (slots - h) % slots if d == 0 else h
        at = grid.at[pl.ds(t * edev + c * ce, ce), rows]
        return remote(
            at, at, s_send.at[j - 1, d, h - 1, c], s_recv.at[j - 1, d, h - 1, c],
            {"kz": lax.rem(k + j, nk)},
        )

    def share_arrival(j, d, h, c):
        source = lax.rem(k + nk - j, nk)
        return share_copy(j, d, h, c, pl.ds(pl.multiple_of(source * half, half), half))

    def x_copy(j, c):
        return remote(
            grid.at[pl.ds(REACH * edev + c * ce, ce), my_rows], other.at[j - 1, pl.ds(c * ce, ce), my_rows],
            x_send.at[j - 1, c], x_recv.at[j - 1, c], {"atom": lax.rem(a + j, na)},
        )

    def xs_copy(j, i, c, rows):
        at = other.at[j - 1, pl.ds(c * ce, ce), rows]
        return remote(
            at, at, xs_send.at[j - 1, i - 1, c], xs_recv.at[j - 1, i - 1, c], {"kz": lax.rem(k + i, nk)}
        )

    def xs_arrival(j, i, c):
        source = lax.rem(k + nk - i, nk)
        return xs_copy(j, i, c, pl.ds(pl.multiple_of(source * half, half), half))

    def far_here(d):
        if d == 0:
            return jnp.logical_and(p >= REACH, p + 1 < ne)
        return jnp.logical_and(p + REACH < ne, p >= 1)

    for j in range(1, na):
        tab_copy(j).start()
    for c in range(chunks):
        raw_copy(c).wait()
        for e in range(c * ce, (c + 1) * ce):
            total = raw[0, e]
            for i in range(1, mom):
                total = total + raw[i, e]
            mine[e] = total
        for j in range(1, nk):
            k_copy(j, c).start()
    for c in range(chunks):
        for j in range(1, nk):
            k_copy(j, c).wait_recv()
        for e in range(c * ce, (c + 1) * ce):
            total = mine[e]
            for j in range(1, nk):
                total = total + theirs[j - 1, e]
            grid[e] = total
        for d in range(2):
            when(sends(d, 1), lambda d=d, c=c: z_copy(d, 1, c).start())

    tab_local.wait()
    for j in range(1, na):
        tab_arrival(j).wait_recv()
    for m in range(MODES):
        owner = owners[m]
        high, low = split(table[owner].T)
        cth[m] = high
        ctl[m] = low
        high, low = split(table[owner, :, pl.ds(pl.multiple_of(a * brows, brows), brows)])
        cah[m] = high
        cal[m] = low
        if far:
            for j in range(na):
                columns = pl.ds(pl.multiple_of(lax.rem(a + na - j, na) * brows, brows), brows)
                rows = pl.ds(pl.multiple_of(a * brows, brows), brows)
                high, low = split(table[owner, rows, columns])
                crh[m * na + j] = high
                crl[m * na + j] = low

    for h in range(1, hops + 1):
        for c in range(chunks):
            for d in range(2):

                def arrived(d=d, h=h, c=c):
                    z_copy(d, h, c).wait_recv()
                    for j in range(1, nk):
                        share_copy(j, d, h, c, my_rows).start()

                when(receives(d, h), arrived)
                if far and h == hops:

                    def spread(c=c):
                        for j in range(1, na):
                            x_copy(j, c).start()

                    pl.when(far_here(d))(spread)
                if h < hops:
                    when(sends(d, h + 1), lambda d=d, h=h, c=c: z_copy(d, h + 1, c).start())
    if far:

        def pass_on(first, last):
            for c in range(first, last):
                for j in range(1, na):
                    x_copy(j, c).wait_recv()
                    for i in range(1, nk):
                        xs_copy(j, i, c, my_rows).start()

        late = max(chunks - 2, 0)
        pl.when(beside_end)(lambda: pass_on(0, late))

    for h in range(1, hops + 1):
        for c in range(chunks):
            for d in range(2):
                for j in range(1, nk):
                    when(receives(d, h), lambda j=j, d=d, h=h, c=c: share_arrival(j, d, h, c).wait_recv())

    span = slots * edev

    def o_copy(j, i):
        q, where = peer(j)
        return remote(
            part.at[i, pl.ds(pl.multiple_of(q * rows_out, rows_out), rows_out)], res.at[me, i],
            o_send.at[j - 1, i], o_recv.at[j - 1, i], where,
        )

    def o_arrival(j, i):
        source = lax.rem(me + peers - j, peers)
        return remote(
            part.at[i, pl.ds(0, rows_out)], res.at[source, i],
            o_send.at[j - 1, i], o_recv.at[j - 1, i], peer(j)[1],
        )

    def o_local(i):
        return pltpu.make_async_copy(
            part.at[i, pl.ds(pl.multiple_of(me * rows_out, rows_out), rows_out)], res.at[me, i], o_sem.at[i]
        )

    def f_copy(j, i):
        q = lax.rem(k + j, nk)
        return remote(
            fpart.at[i, pl.ds(pl.multiple_of(q * rows_out, rows_out), rows_out)], ends.at[k, i],
            f_send.at[j, i], f_recv.at[j, i], {"energy": partner, "kz": q},
        )

    def f_arrival(j, i):
        return remote(
            fpart.at[i, pl.ds(0, rows_out)], ends.at[lax.rem(k + nk - j, nk), i],
            f_send.at[j, i], f_recv.at[j, i], {"energy": partner, "kz": lax.rem(k + j, nk)},
        )

    if far:
        missing = jnp.where(p < 1, slots - 1, jnp.where(p + 1 >= ne, 1, -1))

    def seen(index, e, weight):
        if not far:
            return index, weight
        absent = lax.div(index, edev) == missing
        return jnp.where(absent, e, index), jnp.where(absent, 0.0, weight)

    def near(i):
        e = k * emine + i
        for m in range(MODES):
            weight, step = occ[m], offs[m]
            iu, wu = seen(lax.rem(e + step, span), e, 1.0 + weight)
            il, wl = seen(lax.rem(e - step + span, span), e, weight)
            combined = (wu * grid[iu] + wl * grid[il]) / momenta
            product = dot3(split(combined), (cth[m], ctl[m]))
            term = dot3((cah[m], cal[m]), split(product))
            if m == 0:
                part[i] = term
            else:
                part[i] += term
        for j in range(1, peers):
            o_copy(j, i).start()
        o_local(i).start()

    def among(index, weight):
        inside = index < edev
        return jnp.where(inside, index, 0), jnp.where(inside, weight, 0.0)

    def farthest(i):
        e = (ne - 1) * (2 * p - ne + 1) * edev + span + k * emine + i
        for m in range(MODES):
            weight, step = occ[m], offs[m]
            iu, wu = among(lax.rem(e + step, span), 1.0 + weight)
            il, wl = among(lax.rem(e - step + span, span), weight)
            rows = None
            for j in range(na):
                if j == 0:
                    upper, lower = grid[REACH * edev + iu], grid[REACH * edev + il]
                else:
                    upper, lower = other[j - 1, iu], other[j - 1, il]
                combined = (wu * upper + wl * lower) / momenta
                term = dot3((crh[m * na + j], crl[m * na + j]), split(combined))
                rows = term if rows is None else rows + term
            term = dot3(split(rows), (cth[m], ctl[m]))
            if m == 0:
                fpart[i] = term
            else:
                fpart[i] += term
        for j in range(nk):
            f_copy(j, i).start()

    for i in range(emine):
        near(i)
        if far:

            @pl.when(beside_end)
            def _():
                if i == 0:
                    pass_on(late, chunks)
                    for c in range(chunks):
                        for j in range(1, na):
                            for t in range(1, nk):
                                xs_arrival(j, t, c).wait_recv()
                farthest(i)

    for j in range(1, na):
        tab_copy(j).wait_send()
    for c in range(chunks):
        for j in range(1, nk):
            k_copy(j, c).wait_send()
        for h in range(1, hops + 1):
            for d in range(2):
                when(sends(d, h), lambda d=d, h=h, c=c: z_copy(d, h, c).wait_send())
                for j in range(1, nk):
                    when(receives(d, h), lambda j=j, d=d, h=h, c=c: share_copy(j, d, h, c, my_rows).wait_send())
    if far:

        @pl.when(beside_end)
        def _():
            for c in range(chunks):
                for j in range(1, na):
                    x_copy(j, c).wait_send()
                    for i in range(1, nk):
                        xs_copy(j, i, c, my_rows).wait_send()
            for i in range(emine):
                for j in range(nk):
                    f_copy(j, i).wait_send()

        @pl.when(at_end)
        def _():
            for i in range(emine):
                for j in range(nk):
                    f_arrival(j, i).wait_recv()

    for i in range(emine):
        o_local(i).wait()
        for j in range(1, peers):
            o_copy(j, i).wait_send()
            o_arrival(j, i).wait_recv()


def shards(green, couplings, occupation, offsets, owners):
    mom, edev, brows, order = green.shape
    ne, na, nk = (lax.axis_size(n) for n in ("energy", "atom", "kz"))
    chunks = math.gcd(edev, 8)
    line = ne <= 2 * REACH
    slots = ne if line else 2 * REACH + 1
    hops = min(ne - 1, REACH)
    emine, rows_out = edev // nk, order // (na * nk)
    far = line and ne - 1 > REACH
    f_edev, f_emine, f_brows = (edev, emine, brows) if far else (8, 8, 128)
    f_modes = MODES if far else 1
    dma = pltpu.SemaphoreType.DMA
    smem = pl.BlockSpec(memory_space=pltpu.SMEM)
    hbm = pl.BlockSpec(memory_space=pl.ANY)
    parts, finished = pl.pallas_call(
        functools.partial(kernel, (ne, na, nk, chunks)),
        out_shape=(
            jax.ShapeDtypeStruct((na * nk, emine, rows_out, order), F32),
            jax.ShapeDtypeStruct((nk, emine, rows_out, order) if far else (8, 128), F32),
        ),
        in_specs=[hbm, hbm, smem, smem, smem],
        out_specs=(hbm, hbm),
        scratch_shapes=[
            pltpu.VMEM((slots * edev, brows, order), F32),
            pltpu.VMEM((mom, edev, brows, order), F32),
            pltpu.VMEM((edev, brows, order), F32),
            pltpu.VMEM((nk - 1, edev, brows, order), F32),
            pltpu.VMEM((couplings.shape[0] * na, order, order), F32),
            pltpu.VMEM((MODES, order, order), BF16),
            pltpu.VMEM((MODES, order, order), BF16),
            pltpu.VMEM((MODES, order, brows), BF16),
            pltpu.VMEM((MODES, order, brows), BF16),
            pltpu.VMEM((emine, order, order), F32),
            pltpu.VMEM((na - 1, f_edev, f_brows, order if far else 128), F32),
            pltpu.VMEM((f_modes * na, f_brows, f_brows), BF16),
            pltpu.VMEM((f_modes * na, f_brows, f_brows), BF16),
            pltpu.VMEM((f_emine, f_brows, order if far else 128), F32),
            dma((chunks,)),
            dma,
            dma((na - 1,)),
            dma((na - 1,)),
            dma((nk - 1, chunks)),
            dma((nk - 1, chunks)),
            dma((2, hops, chunks)),
            dma((2, hops, chunks)),
            dma((nk - 1, 2, hops, chunks)),
            dma((nk - 1, 2, hops, chunks)),
            dma((emine,)),
            dma((na * nk - 1, emine)),
            dma((na * nk - 1, emine)),
            dma((na - 1, chunks)),
            dma((na - 1, chunks)),
            dma((na - 1, nk - 1, chunks)),
            dma((na - 1, nk - 1, chunks)),
            dma((nk, emine)),
            dma((nk, emine)),
        ],
        compiler_params=pltpu.CompilerParams(
            collective_id=0, has_side_effects=True, vmem_limit_bytes=58 << 20
        ),
        cost_estimate=pl.CostEstimate(
            flops=12 * MODES * emine * 2 * brows * order * order,
            bytes_accessed=4 * (mom * edev * brows * order + couplings.size + na * nk * emine * rows_out * order),
            transcendentals=0,
        ),
    )(green, couplings, occupation, offsets, owners)
    sigma = jnp.sum(parts.reshape(na, edev, rows_out, order), axis=0)
    if far:
        place = lax.axis_index("energy")
        end = jnp.logical_or(place == 0, place == ne - 1)
        sigma = sigma + jnp.where(end, finished.reshape(edev, rows_out, order), 0.0)
    return jnp.swapaxes(sigma, 0, 1)


def solution(mesh):
    return jax.shard_map(
        shards,
        mesh=mesh,
        in_specs=(P(("grp", "kz"), "energy", "atom", None), P("atom", None, None), P(), P(), P()),
        out_specs=P(("grp", "atom", "kz"), "energy", None),
        check_vma=False,
    )
```
